256 devices in a mesh: tm: 16 (over x, y_lo, core), patch: 16 (over z, y_hi).
Axes of the slice: x: 4, y: 4 (y_hi: 2, y_lo: 2; y = y_hi * 2 + y_lo), z: 8, core: 2. Of those that a mesh axis runs over, the one named last changes fastest.
Arguments:
- queries: bfloat16 [1, 64, 1024, 1024], P(None, 'tm', 'patch'), may hold values from -36 to 36
- key_vectors: bfloat16 [1, 64, 1024, 1024], P(None, 'tm', 'patch'), may hold values from -36 to 36
- value_vectors: bfloat16 [1, 64, 1024, 1024], P(None, 'tm', 'patch'), may hold values from -6 to 6
- grad_output: bfloat16 [1, 64, 1024, 1024], P(None, 'tm', 'patch'), may hold values from -6 to 6
- window_start: int32 [64], replicated, may hold values from 0 to 48, as said below
Outputs:
- attended: bfloat16 [1, 64, 1024, 1024], P(None, 'tm', 'patch')
- grad_queries: bfloat16 [1, 64, 1024, 1024], P(None, 'tm', 'patch')
- grad_keys: bfloat16 [1, 64, 1024, 1024], P(None, 'tm', 'patch')
- grad_values: bfloat16 [1, 64, 1024, 1024], P(None, 'tm', 'patch')
The draws below stay inside these ranges and needn't reach their ends.
Inputs may be any that keep to these rules, and one draw needn't show every extreme that they name: Frame f lies in frames window_start[f] to window_start[f] + 15, and these lie within the clip.
All inputs are finite; a program needn't handle non-finite values.
Results may differ from the reference program's by a relative error of at most 0.015.
Values may be sent and summed in bfloat16 or wider, within the bound.
A program may use at most 128 MiB of HBM per device.

```python
import jax
import jax.numpy as jnp
from jax import lax

HEADS = 16
HD = 64
D = 1024
CLIPS = 1
WINDOW = 16
FRAMES = 64
PATCHES = 1024


def draw_queries(key, part):
    own_key = jax.random.fold_in(key, 1)
    shape_all = (CLIPS, FRAMES, PATCHES, D)
    return jnp.clip(jax.random.normal(own_key, shape_all, jnp.float32), -6.0, 6.0).astype(jnp.bfloat16)


def draw_key_vectors(key, part):
    own_key = jax.random.fold_in(key, 2)
    shape_all = (CLIPS, FRAMES, PATCHES, D)
    return jnp.clip(jax.random.normal(own_key, shape_all, jnp.float32), -6.0, 6.0).astype(jnp.bfloat16)


def draw_window_start(key, part):
    own_key = jax.random.fold_in(key, 3)
    frame_ids = jnp.arange(FRAMES, dtype=jnp.int32)
    lowest = jnp.maximum(frame_ids - (WINDOW - 1), 0)
    highest = jnp.minimum(frame_ids, FRAMES - WINDOW)
    random_ints = jax.random.randint(own_key, (FRAMES,), 0, 1 << 20, dtype=jnp.int32)
    return lowest + random_ints % (highest - lowest + 1)


def shard_levels(rng, extent, pieces, low, largest):
    factor_of = 1.0
    for dim, shards_of in pieces:
        steps = jax.random.uniform(jax.random.fold_in(jax.random.fold_in(rng, 6), dim), (shards_of,), jnp.float32, low / len(pieces), largest / len(pieces))
        factor_of = factor_of * jnp.repeat(jnp.exp(steps), extent[dim] // shards_of).reshape((-1,) + (1,) * (len(extent) - 1 - dim))
    return factor_of


def noise(key, extent, deviation, bound, cuts=(), kind=jnp.bfloat16):
    entries = jax.random.normal(key, extent, jnp.float32) * deviation
    if len(cuts) > 0:
        entries = shard_levels(key, extent, cuts, -0.22, 0.18) * entries
    return jnp.clip(entries, min=-bound, max=bound).astype(kind)


def setup_inputs(seed: int = 0) -> dict:
    splits = jax.random.split(jax.random.key(seed), 6)
    return {
        "queries": draw_queries(jax.random.fold_in(splits[5], 71), 0),
        "key_vectors": draw_key_vectors(jax.random.fold_in(splits[5], 71), 0),
        "value_vectors": noise(splits[2], (CLIPS, FRAMES, PATCHES, D), 1.0, 6.0, ((1, 16), (2, 16))),
        "grad_output": noise(splits[3], (CLIPS, FRAMES, PATCHES, D), 1.0, 6.0, ((1, 16), (2, 16))),
        "window_start": draw_window_start(jax.random.fold_in(splits[5], 71), 0),
    }


def attention_core(queries, key_rows, value_rows, grad_rows, allowed):
    scaling = queries.shape[-1] ** -0.5
    top = lax.Precision.HIGHEST
    query_wide = queries.astype(jnp.float32)
    key_wide = key_rows.astype(jnp.float32)
    value_wide = value_rows.astype(jnp.float32)
    grad_wide = grad_rows.astype(jnp.float32)
    scores = jnp.einsum('bqphd,bkphd->bphqk', query_wide, key_wide, precision=top) * scaling
    if allowed is not None:
        scores = jnp.where(allowed, scores, -1e30)
    highest = jnp.max(scores, axis=-1, keepdims=True)
    exponent = jnp.exp(scores - highest)
    weights = exponent / jnp.sum(exponent, axis=-1, keepdims=True)
    weights_b = weights.astype(jnp.bfloat16).astype(jnp.float32)
    attended = jnp.einsum('bphqk,bkphd->bqphd', weights_b, value_wide, precision=top).astype(jnp.bfloat16)
    weight_grad = jnp.einsum('bqphd,bkphd->bphqk', grad_wide, value_wide, precision=top)
    score_grad = weights * (weight_grad - jnp.sum(weights * weight_grad, axis=-1, keepdims=True))
    score_grad_b = score_grad.astype(jnp.bfloat16).astype(jnp.float32)
    grad_queries = jnp.einsum('bphqk,bkphd->bqphd', score_grad_b, key_wide, precision=top) * scaling
    grad_keys = jnp.einsum('bphqk,bqphd->bkphd', score_grad_b, query_wide, precision=top) * scaling
    grad_values = jnp.einsum('bphqk,bqphd->bkphd', weights_b, grad_wide, precision=top)
    return (attended, grad_queries.astype(jnp.bfloat16), grad_keys.astype(jnp.bfloat16),
            grad_values.astype(jnp.bfloat16))


def reference(queries, key_vectors, value_vectors, grad_output, window_start):
    half_width = D // 2
    inputs = (queries, key_vectors, value_vectors, grad_output)

    def spatial_frame(item):
        return attention_core(item[0], item[1], item[2], item[3], None)

    spatial_in = tuple(tensor[..., :half_width].reshape(CLIPS * FRAMES, 1, PATCHES, 1, HEADS // 2, HD)
                       for tensor in inputs)
    spatial_res = lax.map(spatial_frame, spatial_in)
    spatial_out = [tensor.reshape(CLIPS, FRAMES, PATCHES, half_width) for tensor in spatial_res]

    frame_ids = jnp.arange(FRAMES, dtype=jnp.int32)
    allowed = (frame_ids[None, :] >= window_start[:, None]) & (frame_ids[None, :] < window_start[:, None] + WINDOW)

    def temporal_clip(item):
        return attention_core(item[0], item[1], item[2], item[3], allowed)

    temporal_in = tuple(tensor[..., half_width:].reshape(CLIPS, 1, FRAMES, PATCHES, HEADS // 2, HD)
                        for tensor in inputs)
    temporal_res = lax.map(temporal_clip, temporal_in)
    temporal_out = [tensor.reshape(CLIPS, FRAMES, PATCHES, half_width) for tensor in temporal_res]
    joined = [jnp.concatenate([spatial_out[index], temporal_out[index]], axis=-1) for index in range(4)]
    return (joined[0], joined[1], joined[2], joined[3])
```

```python
import functools

import jax
import jax.numpy as jnp
from jax import lax
from jax.experimental import pallas as pl
from jax.experimental.pallas import tpu as pltpu
from jax.sharding import PartitionSpec as P

MESH = pl.DeviceIdType.MESH
BF16 = jnp.bfloat16
F32 = jnp.float32
N = 16
FR = 4
PT = 64
WINDOW = 16
SCALE = 0.125
QB = 256


def dot(a, b, ca, cb):
    return lax.dot_general(a, b, (((ca,), (cb,)), ((), ())), preferred_element_type=F32)


def kernel(
    q_hbm, k_hbm, v_hbm, g_hbm, ws_ref,
    o_ref, dq_ref, dk_ref, dv_ref,
    inp, s_send, t_send, s_in, t_in, t_f32, tr_a, acc, s_out, s_back, t_back,
    in_sem, ss_sem, sr_sem, ts_sem, tr_sem, bs_sem, br_sem, us_sem, ur_sem,
):
    me_t = lax.axis_index("tm")
    me_p = lax.axis_index("patch")

    def patch_peer(j):
        z = (me_p // 2 + j // 2) % 8
        y = (me_p % 2 + j % 2) % 2
        return z * 2 + y

    def tm_peer(j):
        return (me_t + j) % N

    def to_patch(d):
        return (me_t, d)

    def to_tm(e):
        return (e, me_p)

    loads = []
    for half in range(2):
        for a, ref in enumerate((q_hbm, k_hbm, v_hbm, g_hbm)):
            cols = pl.ds(half * 512, 512)
            copy = pltpu.make_async_copy(
                ref.at[0, :, :, cols], inp.at[a, :, :, cols], in_sem.at[half, a]
            )
            copy.start()
            loads.append(copy)

    barrier = pltpu.get_barrier_semaphore()

    def greet(j, carry):
        pl.semaphore_signal(barrier, inc=1, device_id=to_patch(patch_peer(j)), device_id_type=MESH)
        pl.semaphore_signal(barrier, inc=1, device_id=to_tm(tm_peer(j)), device_id_type=MESH)
        return carry

    lax.fori_loop(1, N, greet, 0)

    def pack_spatial(d):
        f = d // 4
        cols = pl.ds(pl.multiple_of((d % 4) * 128, 128), 128)
        q, k, v, g = (inp[a, f, :, cols] for a in range(4))
        out = []
        for c in range(2):
            h = slice(c * 64, c * 64 + 64)
            out.append(jnp.concatenate([q[:, h], g[:, h]], axis=1))
            out.append(jnp.concatenate([k[:, h], v[:, h]], axis=1))
        return out

    for copy in loads[:4]:
        copy.wait()

    def fill_spatial(j, carry):
        d = patch_peer(j)
        parts = pack_spatial(d)
        for c in range(2):
            for s in range(2):
                s_send[d, c, s] = parts[2 * c + s]
        return carry

    lax.fori_loop(1, N, fill_spatial, 0)
    parts = pack_spatial(me_p)
    own_rows = pl.ds(pl.multiple_of(me_p * PT, PT), PT)
    for c in range(2):
        for s in range(2):
            s_in[c, s, own_rows, :] = parts[2 * c + s]

    pl.semaphore_wait(barrier, 2 * (N - 1))

    def s_copy(c, d):
        return pltpu.make_async_remote_copy(
            src_ref=s_send.at[d, c],
            dst_ref=s_in.at[c, :, own_rows, :],
            send_sem=ss_sem.at[c, d],
            recv_sem=sr_sem.at[c, me_p],
            device_id=to_patch(d),
            device_id_type=MESH,
        )

    def s_arrival(c, d):
        return pltpu.make_async_remote_copy(
            src_ref=s_send.at[d, c],
            dst_ref=s_in.at[c, :, pl.ds(pl.multiple_of(d * PT, PT), PT), :],
            send_sem=ss_sem.at[c, d],
            recv_sem=sr_sem.at[c, d],
            device_id=to_patch(d),
            device_id_type=MESH,
        )

    def t_copy(e):
        return pltpu.make_async_remote_copy(
            src_ref=t_send.at[0, e],
            dst_ref=t_in.at[me_t],
            send_sem=ts_sem.at[e],
            recv_sem=tr_sem.at[me_t],
            device_id=to_tm(e),
            device_id_type=MESH,
        )

    def t_arrival(e):
        return pltpu.make_async_remote_copy(
            src_ref=t_send.at[0, e],
            dst_ref=t_in.at[e],
            send_sem=ts_sem.at[e],
            recv_sem=tr_sem.at[e],
            device_id=to_tm(e),
            device_id_type=MESH,
        )

    def b_copy(c, d):
        return pltpu.make_async_remote_copy(
            src_ref=s_out.at[c, :, pl.ds(pl.multiple_of(d * PT, PT), PT), :],
            dst_ref=s_back.at[me_p, c],
            send_sem=bs_sem.at[c, d],
            recv_sem=br_sem.at[c, me_p],
            device_id=to_patch(d),
            device_id_type=MESH,
        )

    def b_arrival(c, d):
        return pltpu.make_async_remote_copy(
            src_ref=s_out.at[c, :, pl.ds(pl.multiple_of(d * PT, PT), PT), :],
            dst_ref=s_back.at[d, c],
            send_sem=bs_sem.at[c, d],
            recv_sem=br_sem.at[c, d],
            device_id=to_patch(d),
            device_id_type=MESH,
        )

    def u_copy(e):
        return pltpu.make_async_remote_copy(
            src_ref=t_send.at[1, e],
            dst_ref=t_back.at[me_t],
            send_sem=us_sem.at[e],
            recv_sem=ur_sem.at[me_t],
            device_id=to_tm(e),
            device_id_type=MESH,
        )

    def u_arrival(e):
        return pltpu.make_async_remote_copy(
            src_ref=t_send.at[1, e],
            dst_ref=t_back.at[e],
            send_sem=us_sem.at[e],
            recv_sem=ur_sem.at[e],
            device_id=to_tm(e),
            device_id_type=MESH,
        )

    def each(peer, act):
        def body(j, carry):
            act(peer(j))
            return carry

        lax.fori_loop(1, N, body, 0)

    each(patch_peer, lambda d: s_copy(0, d).start())

    for copy in loads[4:]:
        copy.wait()

    def pack_temporal(e):
        rows = pl.ds(pl.multiple_of((e // 4) * 16, 16), 16)
        cols = pl.ds(pl.multiple_of(512 + (e % 4) * 128, 128), 128)
        return [inp[a, :, rows, cols] for a in range(4)]

    def send_temporal(e):
        parts = pack_temporal(e)
        for a in range(4):
            t_send[0, e, a] = parts[a]
        t_copy(e).start()

    each(tm_peer, send_temporal)
    each(patch_peer, lambda d: s_copy(1, d).start())
    parts = pack_temporal(me_t)
    for a in range(4):
        t_in[me_t, a] = parts[a]

    def spatial(c):
        each(patch_peer, lambda d: s_arrival(c, d).wait_recv())
        low = lax.broadcasted_iota(jnp.int32, (QB, 128), 1) < 64

        def turn(i, carry):
            rows = pl.ds(pl.multiple_of(i * QB, QB), QB)
            a = s_in[c, 0, rows, :].astype(F32)
            tr_a[:, rows] = jnp.where(low, a * SCALE, a).T.astype(BF16)
            return carry

        lax.fori_loop(0, 1024 // QB, turn, 0)
        acc[...] = jnp.zeros_like(acc)

        def block(i, carry):
            rows = pl.ds(pl.multiple_of(i * QB, QB), QB)
            a = s_in[c, 0, rows, :]
            b = s_in[c, 1]
            zero = jnp.zeros_like(a)
            a_q = jnp.where(low, a * SCALE, zero)
            a_g = jnp.where(low, zero, a)
            scores = dot(a_q, b, 1, 1)
            weight_grad = dot(a_g, b, 1, 1)
            e = jnp.exp(scores - jnp.max(scores, axis=1, keepdims=True))
            w = e * (1.0 / jnp.sum(e, axis=1, keepdims=True))
            delta = jnp.sum(w * weight_grad, axis=1, keepdims=True)
            ds_b = (w * (weight_grad - delta)).astype(BF16)
            w_b = w.astype(BF16)
            out = jnp.where(low, dot(ds_b, b, 1, 0) * SCALE, dot(w_b, b, 1, 0))
            s_out[c, 0, rows, :] = out.astype(BF16)
            acc[0:64, :] += dot(tr_a[0:64, rows], ds_b, 1, 0)
            acc[64:128, :] += dot(tr_a[64:128, rows], w_b, 1, 0)
            return carry

        lax.fori_loop(0, 1024 // QB, block, 0)

        def back(i, carry):
            rows = pl.ds(pl.multiple_of(i * QB, QB), QB)
            s_out[c, 1, rows, :] = acc[:, rows].T.astype(BF16)
            return carry

        lax.fori_loop(0, 1024 // QB, back, 0)
        each(patch_peer, lambda d: b_copy(c, d).start())
        for s in range(2):
            s_back[me_p, c, s] = s_out[c, s, own_rows, :]

    def temporal():
        each(tm_peer, lambda e: t_arrival(e).wait_recv())

        def widen(e, carry):
            for a in range(4):
                rows = pl.ds(pl.multiple_of(e * 64, 64), 64)
                t_f32[a, rows, :] = t_in[e, a].reshape(64, 128).astype(F32)
            return carry

        lax.fori_loop(0, N, widen, 0)
        i0 = lax.broadcasted_iota(jnp.int32, (64, 64), 0)
        i1 = lax.broadcasted_iota(jnp.int32, (64, 64), 1)
        starts = jnp.sum(
            jnp.where(i0 == i1, jnp.broadcast_to(ws_ref[...].astype(F32), (64, 64)), 0.0),
            axis=1, keepdims=True,
        )
        lanes = lax.broadcasted_iota(jnp.int32, (64, 128), 1)
        low = lanes < 64
        frame = jnp.where(low, lanes, lanes - 64).astype(F32)
        allowed = (frame >= starts) & (frame < starts + WINDOW)
        allowed_0 = allowed & low
        allowed_1 = allowed & ~low

        def halves(x, op, fill, mask_0, mask_1):
            r0 = op(jnp.where(mask_0, x, fill), axis=1, keepdims=True)
            r1 = op(jnp.where(mask_1, x, fill), axis=1, keepdims=True)
            return jnp.where(low, r0, r1)

        def one(p):
            rows = pl.ds(p, 64, stride=16)
            q, k, v, g = (t_f32[a, rows, :] for a in range(4))

            def diagonal(x):
                return jnp.concatenate(
                    [jnp.where(low, x, 0.0), jnp.where(low, 0.0, x)], axis=0
                ).astype(BF16)

            q = (q * SCALE).astype(BF16)
            g = g.astype(BF16)
            k_d = diagonal(k)
            v_d = diagonal(v)
            scores = dot(q, k_d, 1, 1)
            weight_grad = dot(g, v_d, 1, 1)
            highest = halves(scores, jnp.max, -1e30, allowed_0, allowed_1)
            e = jnp.where(allowed, jnp.exp(scores - highest), 0.0)
            w = e * (1.0 / halves(e, jnp.sum, 0.0, low, ~low))
            delta = halves(w * weight_grad, jnp.sum, 0.0, low, ~low)
            ds_b = (w * (weight_grad - delta)).astype(BF16)
            w_b = w.astype(BF16)
            o = dot(w_b, v_d, 1, 0)
            dq = dot(ds_b, k_d, 1, 0) * SCALE
            dk = dot(ds_b, q, 0, 0)
            dv = dot(w_b, g, 0, 0)
            dk = jnp.where(low, dk[:64], dk[64:])
            dv = jnp.where(low, dv[:64], dv[64:])
            for a, x in enumerate((o, dq, dk, dv)):
                t_f32[a, rows, :] = x

        def patches(i, carry):
            for u in range(2):
                one(i * 2 + u)
            return carry

        lax.fori_loop(0, 8, patches, 0)

        def narrow(e):
            rows = pl.ds(pl.multiple_of(e * 64, 64), 64)
            return [t_f32[a, rows, :].astype(BF16).reshape(4, 16, 128) for a in range(4)]

        def send_back(e):
            parts = narrow(e)
            for a in range(4):
                t_send[1, e, a] = parts[a]
            u_copy(e).start()

        each(tm_peer, send_back)
        parts = narrow(me_t)
        for a in range(4):
            t_back[me_t, a] = parts[a]

    spatial(0)
    temporal()
    spatial(1)

    outs = (o_ref, dq_ref, dk_ref, dv_ref)

    def unpack_temporal(e):
        rows = pl.ds(pl.multiple_of((e // 4) * 16, 16), 16)
        cols = pl.ds(pl.multiple_of(512 + (e % 4) * 128, 128), 128)
        for a in range(4):
            outs[a][0, :, rows, cols] = t_back[e, a]

    def take_temporal(e):
        u_arrival(e).wait_recv()
        unpack_temporal(e)

    unpack_temporal(me_t)
    each(tm_peer, take_temporal)

    def unpack_spatial(d):
        f = d // 4
        cols = pl.ds(pl.multiple_of((d % 4) * 128, 128), 128)
        for s, (low_ref, high_ref) in enumerate(((dq_ref, o_ref), (dk_ref, dv_ref))):
            x, y = s_back[d, 0, s], s_back[d, 1, s]
            low_ref[0, f, :, cols] = jnp.concatenate([x[:, :64], y[:, :64]], axis=1)
            high_ref[0, f, :, cols] = jnp.concatenate([x[:, 64:], y[:, 64:]], axis=1)

    unpack_spatial(me_p)
    each(patch_peer, lambda d: b_arrival(0, d).wait_recv())

    def take_spatial(d):
        b_arrival(1, d).wait_recv()
        unpack_spatial(d)

    each(patch_peer, take_spatial)

    def drain_patch(d):
        for c in range(2):
            s_copy(c, d).wait_send()
            b_copy(c, d).wait_send()

    def drain_tm(e):
        t_copy(e).wait_send()
        u_copy(e).wait_send()

    each(patch_peer, drain_patch)
    each(tm_peer, drain_tm)


def on_device(queries, key_vectors, value_vectors, grad_output, window_start):
    anywhere = pl.BlockSpec(memory_space=pltpu.HBM)
    vmem = pl.BlockSpec(memory_space=pltpu.VMEM)
    dma = pltpu.SemaphoreType.DMA
    shape = jax.ShapeDtypeStruct((1, FR, PT, 1024), BF16)
    return pl.pallas_call(
        kernel,
        out_shape=(shape,) * 4,
        in_specs=[anywhere] * 4 + [vmem],
        out_specs=(vmem,) * 4,
        scratch_shapes=[
            pltpu.VMEM((4, FR, PT, 1024), BF16),
            pltpu.VMEM((N, 2, 2, PT, 128), BF16),
            pltpu.VMEM((2, N, 4, FR, 16, 128), BF16),
            pltpu.VMEM((2, 2, 1024, 128), BF16),
            pltpu.VMEM((N, 4, FR, 16, 128), BF16),
            pltpu.VMEM((4, 1024, 128), F32),
            pltpu.VMEM((128, 1024), BF16),
            pltpu.VMEM((128, 1024), F32),
            pltpu.VMEM((2, 2, 1024, 128), BF16),
            pltpu.VMEM((N, 2, 2, PT, 128), BF16),
            pltpu.VMEM((N, 4, FR, 16, 128), BF16),
            dma((2, 4)),
            dma((2, N)), dma((2, N)), dma((N,)), dma((N,)),
            dma((2, N)), dma((2, N)), dma((N,)), dma((N,)),
        ],
        compiler_params=pltpu.CompilerParams(
            collective_id=0, has_side_effects=True, vmem_limit_bytes=60 << 20
        ),
        name="attention",
    )(queries, key_vectors, value_vectors, grad_output, window_start.reshape(1, 64))


def solution(mesh):
    spec = P(None, "tm", "patch", None)
    return jax.shard_map(
        on_device,
        mesh=mesh,
        in_specs=(spec,) * 4 + (P(),),
        out_specs=(spec,) * 4,
        check_vma=False,
    )
```

```python
import functools

import jax
import jax.numpy as jnp
from jax import lax
from jax.experimental import pallas as pl
from jax.experimental.pallas import tpu as pltpu
from jax.sharding import PartitionSpec as P

MESH = pl.DeviceIdType.MESH
BF16 = jnp.bfloat16
F32 = jnp.float32
N = 16
FR = 4
PT = 64
WINDOW = 16
SCALE = 0.125
GROUP = 4
QB = 256


def dot(a, b, ca, cb):
    return lax.dot_general(a, b, (((ca,), (cb,)), ((), ())), preferred_element_type=F32)


def kernel(
    q_hbm, k_hbm, v_hbm, g_hbm, ws_hbm,
    o_ref, dq_ref, dk_ref, dv_ref,
    ws_ref, inp, s_send, t_send, s_in, t_in, t_f32, t_res, tr_a, acc, s_out, s_back, t_back,
    ws_sem, in_sem, ss_sem, sr_sem, ts_sem, tr_sem, bs_sem, br_sem, us_sem, ur_sem,
):
    me_t = lax.axis_index("tm")
    me_p = lax.axis_index("patch")

    def patch_peer(j):
        z = (me_p // 2 + j // 2) % 8
        y = (me_p % 2 + j % 2) % 2
        return z * 2 + y

    def tm_peer(j):
        return (me_t + j) % N

    def to_patch(d):
        return (me_t, d)

    def to_tm(e):
        return (e, me_p)

    loads = []
    for half in range(2):
        for a, ref in enumerate((q_hbm, k_hbm, v_hbm, g_hbm)):
            cols = pl.ds(half * 512, 512)
            copy = pltpu.make_async_copy(
                ref.at[0, :, :, cols], inp.at[a, :, :, cols], in_sem.at[half, a]
            )
            copy.start()
            loads.append(copy)

    ws_copy = pltpu.make_async_copy(ws_hbm, ws_ref, ws_sem)
    ws_copy.start()

    barrier = pltpu.get_barrier_semaphore()

    def greet(j, carry):
        pl.semaphore_signal(barrier, inc=1, device_id=to_patch(patch_peer(j)), device_id_type=MESH)
        pl.semaphore_signal(barrier, inc=1, device_id=to_tm(tm_peer(j)), device_id_type=MESH)
        return carry

    lax.fori_loop(1, N, greet, 0)

    def pack_spatial(c, d):
        f = d // 4
        cols = pl.ds(pl.multiple_of((d % 4) * 128, 128), 128)
        q, k, v, g = (inp[a, f, :, cols] for a in range(4))
        h = slice(c * 64, c * 64 + 64)
        return (
            jnp.concatenate([q[:, h], g[:, h]], axis=1),
            jnp.concatenate([k[:, h], v[:, h]], axis=1),
        )

    own_rows = pl.ds(pl.multiple_of(me_p * PT, PT), PT)

    def s_copy(c, d):
        return pltpu.make_async_remote_copy(
            src_ref=s_send.at[d, c],
            dst_ref=s_in.at[c, :, own_rows, :],
            send_sem=ss_sem.at[c, d],
            recv_sem=sr_sem.at[c, me_p],
            device_id=to_patch(d),
            device_id_type=MESH,
        )

    def s_arrival(c, d):
        return pltpu.make_async_remote_copy(
            src_ref=s_send.at[d, c],
            dst_ref=s_in.at[c, :, pl.ds(pl.multiple_of(d * PT, PT), PT), :],
            send_sem=ss_sem.at[c, d],
            recv_sem=sr_sem.at[c, d],
            device_id=to_patch(d),
            device_id_type=MESH,
        )

    def t_copy(e):
        return pltpu.make_async_remote_copy(
            src_ref=t_send.at[0, e],
            dst_ref=t_in.at[me_t],
            send_sem=ts_sem.at[e],
            recv_sem=tr_sem.at[me_t],
            device_id=to_tm(e),
            device_id_type=MESH,
        )

    def t_arrival(e):
        return pltpu.make_async_remote_copy(
            src_ref=t_send.at[0, e],
            dst_ref=t_in.at[e],
            send_sem=ts_sem.at[e],
            recv_sem=tr_sem.at[e],
            device_id=to_tm(e),
            device_id_type=MESH,
        )

    def b_copy(c, d):
        return pltpu.make_async_remote_copy(
            src_ref=s_out.at[c, :, pl.ds(pl.multiple_of(d * PT, PT), PT), :],
            dst_ref=s_back.at[me_p, c],
            send_sem=bs_sem.at[c, d],
            recv_sem=br_sem.at[c, me_p],
            device_id=to_patch(d),
            device_id_type=MESH,
        )

    def b_arrival(c, d):
        return pltpu.make_async_remote_copy(
            src_ref=s_out.at[c, :, pl.ds(pl.multiple_of(d * PT, PT), PT), :],
            dst_ref=s_back.at[d, c],
            send_sem=bs_sem.at[c, d],
            recv_sem=br_sem.at[c, d],
            device_id=to_patch(d),
            device_id_type=MESH,
        )

    def u_copy(e):
        return pltpu.make_async_remote_copy(
            src_ref=t_send.at[1, e],
            dst_ref=t_back.at[me_t],
            send_sem=us_sem.at[e],
            recv_sem=ur_sem.at[me_t],
            device_id=to_tm(e),
            device_id_type=MESH,
        )

    def u_arrival(e):
        return pltpu.make_async_remote_copy(
            src_ref=t_send.at[1, e],
            dst_ref=t_back.at[e],
            send_sem=us_sem.at[e],
            recv_sem=ur_sem.at[e],
            device_id=to_tm(e),
            device_id_type=MESH,
        )

    def each(peer, act):
        def body(j, carry):
            act(peer(j))
            return carry

        lax.fori_loop(1, N, body, 0)

    for copy in loads[:4]:
        copy.wait()
    pl.semaphore_wait(barrier, 2 * (N - 1))

    def send_spatial(c):
        def act(d):
            parts = pack_spatial(c, d)
            for s in range(2):
                s_send[d, c, s] = parts[s]
            s_copy(c, d).start()

        each(patch_peer, act)

    send_spatial(0)
    for copy in loads[4:]:
        copy.wait()

    def pack_temporal(e):
        rows = pl.ds(pl.multiple_of((e // 4) * 16, 16), 16)
        cols = pl.ds(pl.multiple_of(512 + (e % 4) * 128, 128), 128)
        return [inp[a, :, rows, cols] for a in range(4)]

    def send_temporal(e):
        parts = pack_temporal(e)
        for a in range(4):
            t_send[0, e, a] = parts[a]
        t_copy(e).start()

    each(tm_peer, send_temporal)
    send_spatial(1)
    for c in range(2):
        parts = pack_spatial(c, me_p)
        for s in range(2):
            s_in[c, s, own_rows, :] = parts[s]
    parts = pack_temporal(me_t)
    for a in range(4):
        t_in[me_t, a] = parts[a]

    def spatial(c):
        each(patch_peer, lambda d: s_arrival(c, d).wait_recv())
        low = lax.broadcasted_iota(jnp.int32, (QB, 128), 1) < 64

        def turn(i, carry):
            rows = pl.ds(pl.multiple_of(i * QB, QB), QB)
            a = s_in[c, 0, rows, :].astype(F32)
            tr_a[:, rows] = jnp.where(low, a * SCALE, a).T.astype(BF16)
            return carry

        lax.fori_loop(0, 1024 // QB, turn, 0)
        acc[...] = jnp.zeros_like(acc)

        def block(i, carry):
            rows = pl.ds(pl.multiple_of(i * QB, QB), QB)
            a = s_in[c, 0, rows, :]
            b = s_in[c, 1]
            zero = jnp.zeros_like(a)
            a_q = jnp.where(low, a * SCALE, zero)
            a_g = jnp.where(low, zero, a)
            scores = dot(a_q, b, 1, 1)
            weight_grad = dot(a_g, b, 1, 1)
            e = jnp.exp(scores - jnp.max(scores, axis=1, keepdims=True))
            w = e * (1.0 / jnp.sum(e, axis=1, keepdims=True))
            delta = jnp.sum(w * weight_grad, axis=1, keepdims=True)
            ds_b = (w * (weight_grad - delta)).astype(BF16)
            w_b = w.astype(BF16)
            out = jnp.where(low, dot(ds_b, b, 1, 0) * SCALE, dot(w_b, b, 1, 0))
            s_out[c, 0, rows, :] = out.astype(BF16)
            acc[0:64, :] += dot(tr_a[0:64, rows], ds_b, 1, 0)
            acc[64:128, :] += dot(tr_a[64:128, rows], w_b, 1, 0)
            return carry

        lax.fori_loop(0, 1024 // QB, block, 0)

        def back(i, carry):
            rows = pl.ds(pl.multiple_of(i * QB, QB), QB)
            s_out[c, 1, rows, :] = acc[:, rows].T.astype(BF16)
            return carry

        lax.fori_loop(0, 1024 // QB, back, 0)
        each(patch_peer, lambda d: b_copy(c, d).start())
        for s in range(2):
            s_back[me_p, c, s] = s_out[c, s, own_rows, :]

    def temporal():
        ws_copy.wait()
        each(tm_peer, lambda e: t_arrival(e).wait_recv())

        def widen(e, carry):
            for a in range(4):
                rows = pl.ds(pl.multiple_of(e * 64, 64), 64)
                t_f32[a, rows, :] = t_in[e, a].reshape(64, 128).astype(F32)
            return carry

        lax.fori_loop(0, N, widen, 0)
        i0 = lax.broadcasted_iota(jnp.int32, (64, 64), 0)
        i1 = lax.broadcasted_iota(jnp.int32, (64, 64), 1)
        starts = jnp.sum(
            jnp.where(i0 == i1, jnp.broadcast_to(ws_ref[...].astype(F32), (64, 64)), 0.0),
            axis=1, keepdims=True,
        )
        lanes = lax.broadcasted_iota(jnp.int32, (64, 128), 1)
        low = lanes < 64
        frame = jnp.where(low, lanes, lanes - 64).astype(F32)
        allowed = (frame >= starts) & (frame < starts + WINDOW)
        allowed_0 = allowed & low
        allowed_1 = allowed & ~low

        def halves(x, op, fill, mask_0, mask_1):
            r0 = op(jnp.where(mask_0, x, fill), axis=1, keepdims=True)
            r1 = op(jnp.where(mask_1, x, fill), axis=1, keepdims=True)
            return jnp.where(low, r0, r1)

        def diagonal(x):
            return jnp.concatenate(
                [jnp.where(low, x, 0.0), jnp.where(low, 0.0, x)], axis=0
            ).astype(BF16)

        def patches(i, carry):
            group = [pl.ds(i * GROUP + u, 64, stride=16) for u in range(GROUP)]
            items = []
            for rows in group:
                q, k, v, g = (t_f32[a, rows, :] for a in range(4))
                items.append(((q * SCALE).astype(BF16), diagonal(k), diagonal(v), g.astype(BF16)))
            scores = [dot(q, k_d, 1, 1) for q, k_d, v_d, g in items]
            weight_grads = [dot(g, v_d, 1, 1) for q, k_d, v_d, g in items]
            highest = [halves(x, jnp.max, -1e30, allowed_0, allowed_1) for x in scores]
            exps = [
                jnp.where(allowed, jnp.exp(x - m), 0.0) for x, m in zip(scores, highest)
            ]
            ws = [e * (1.0 / halves(e, jnp.sum, 0.0, low, ~low)) for e in exps]
            deltas = [
                halves(w * x, jnp.sum, 0.0, low, ~low) for w, x in zip(ws, weight_grads)
            ]
            grads = [
                (w * (x - m)).astype(BF16) for w, x, m in zip(ws, weight_grads, deltas)
            ]
            ws = [w.astype(BF16) for w in ws]
            for rows, (q, k_d, v_d, g), w_b, ds_b in zip(group, items, ws, grads):
                dk = dot(ds_b, q, 0, 0)
                dv = dot(w_b, g, 0, 0)
                t_res[0, rows, :] = dot(w_b, v_d, 1, 0)
                t_res[1, rows, :] = dot(ds_b, k_d, 1, 0) * SCALE
                t_res[2, rows, :] = jnp.where(low, dk[:64], dk[64:])
                t_res[3, rows, :] = jnp.where(low, dv[:64], dv[64:])
            return carry

        lax.fori_loop(0, 16 // GROUP, patches, 0)

        def narrow(e):
            rows = pl.ds(pl.multiple_of(e * 64, 64), 64)
            return [t_res[a, rows, :].astype(BF16).reshape(4, 16, 128) for a in range(4)]

        def send_back(e):
            parts = narrow(e)
            for a in range(4):
                t_send[1, e, a] = parts[a]
            u_copy(e).start()

        each(tm_peer, send_back)
        parts = narrow(me_t)
        for a in range(4):
            t_back[me_t, a] = parts[a]

    spatial(0)
    temporal()
    spatial(1)

    outs = (o_ref, dq_ref, dk_ref, dv_ref)

    def unpack_temporal(e):
        rows = pl.ds(pl.multiple_of((e // 4) * 16, 16), 16)
        cols = pl.ds(pl.multiple_of(512 + (e % 4) * 128, 128), 128)
        for a in range(4):
            outs[a][0, :, rows, cols] = t_back[e, a]

    def take_temporal(e):
        u_arrival(e).wait_recv()
        unpack_temporal(e)

    unpack_temporal(me_t)
    each(tm_peer, take_temporal)

    def unpack_spatial(d):
        f = d // 4
        cols = pl.ds(pl.multiple_of((d % 4) * 128, 128), 128)
        for s, (low_ref, high_ref) in enumerate(((dq_ref, o_ref), (dk_ref, dv_ref))):
            x, y = s_back[d, 0, s], s_back[d, 1, s]
            low_ref[0, f, :, cols] = jnp.concatenate([x[:, :64], y[:, :64]], axis=1)
            high_ref[0, f, :, cols] = jnp.concatenate([x[:, 64:], y[:, 64:]], axis=1)

    unpack_spatial(me_p)
    each(patch_peer, lambda d: b_arrival(0, d).wait_recv())

    def drain_patch(d):
        for c in range(2):
            s_copy(c, d).wait_send()
        b_copy(0, d).wait_send()

    def drain_tm(e):
        t_copy(e).wait_send()
        u_copy(e).wait_send()

    each(patch_peer, drain_patch)
    each(tm_peer, drain_tm)

    def take_spatial(d):
        b_arrival(1, d).wait_recv()
        b_copy(1, d).wait_send()
        unpack_spatial(d)

    each(patch_peer, take_spatial)


def emit(*refs):
    sem = refs[8]
    copies = [
        pltpu.make_async_copy(src, dst, sem.at[a])
        for a, (src, dst) in enumerate(zip(refs[:4], refs[4:8]))
    ]
    for copy in copies:
        copy.start()
    for copy in copies:
        copy.wait()


def on_device(queries, key_vectors, value_vectors, grad_output, window_start):
    anywhere = pl.BlockSpec(memory_space=pltpu.HBM)
    vmem = pl.BlockSpec(memory_space=pltpu.VMEM)
    dma = pltpu.SemaphoreType.DMA
    shape = jax.ShapeDtypeStruct((1, FR, PT, 1024), BF16)
    results = pl.pallas_call(
        kernel,
        out_shape=(shape,) * 4,
        in_specs=[anywhere] * 5,
        out_specs=(vmem,) * 4,
        scratch_shapes=[
            pltpu.VMEM((1, 64), jnp.int32),
            pltpu.VMEM((4, FR, PT, 1024), BF16),
            pltpu.VMEM((N, 2, 2, PT, 128), BF16),
            pltpu.VMEM((2, N, 4, FR, 16, 128), BF16),
            pltpu.VMEM((2, 2, 1024, 128), BF16),
            pltpu.VMEM((N, 4, FR, 16, 128), BF16),
            pltpu.VMEM((4, 1024, 128), F32),
            pltpu.VMEM((4, 1024, 128), F32),
            pltpu.VMEM((128, 1024), BF16),
            pltpu.VMEM((128, 1024), F32),
            pltpu.VMEM((2, 2, 1024, 128), BF16),
            pltpu.VMEM((N, 2, 2, PT, 128), BF16),
            pltpu.VMEM((N, 4, FR, 16, 128), BF16),
            dma, dma((2, 4)),
            dma((2, N)), dma((2, N)), dma((N,)), dma((N,)),
            dma((2, N)), dma((2, N)), dma((N,)), dma((N,)),
        ],
        compiler_params=pltpu.CompilerParams(
            collective_id=0, has_side_effects=True, vmem_limit_bytes=52900 << 10
        ),
        name="attention",
    )(queries, key_vectors, value_vectors, grad_output, window_start.reshape(1, 64))
    return pl.pallas_call(
        emit,
        out_shape=(shape,) * 4,
        in_specs=[vmem] * 4,
        out_specs=(anywhere,) * 4,
        scratch_shapes=[dma((4,))],
        compiler_params=pltpu.CompilerParams(vmem_limit_bytes=6 << 20),
        name="emit",
    )(*results)


def solution(mesh):
    spec = P(None, "tm", "patch", None)
    return jax.shard_map(
        on_device,
        mesh=mesh,
        in_specs=(spec,) * 4 + (P(),),
        out_specs=(spec,) * 4,
        check_vma=False,
    )
```

```python
import functools

import jax
import jax.numpy as jnp
from jax import lax
from jax.experimental import pallas as pl
from jax.experimental.pallas import tpu as pltpu
from jax.sharding import PartitionSpec as P

MESH = pl.DeviceIdType.MESH
BF16 = jnp.bfloat16
F32 = jnp.float32
N = 16
FR = 4
PT = 64
WINDOW = 16
SCALE = 0.125
GROUP = 4
QB = 256


def dot(a, b, ca, cb):
    return lax.dot_general(a, b, (((ca,), (cb,)), ((), ())), preferred_element_type=F32)


def kernel(
    q_hbm, k_hbm, v_hbm, g_hbm, ws_hbm,
    o_ref, dq_ref, dk_ref, dv_ref,
    ws_ref, inp, s_send, t_send, s_in, t_in, t_f32, t_res, tr_a, acc, s_out, s_back, t_back,
    ws_sem, in_sem, ss_sem, sr_sem, ts_sem, tr_sem, bs_sem, b0_sem, br_sem, us_sem, ur_sem,
):
    me_t = lax.axis_index("tm")
    me_p = lax.axis_index("patch")

    def patch_peer(j):
        z = (me_p // 2 + j // 2) % 8
        y = (me_p % 2 + j % 2) % 2
        return z * 2 + y

    def tm_peer(j):
        return (me_t + j) % N

    def to_patch(d):
        return (me_t, d)

    def to_tm(e):
        return (e, me_p)

    barrier = pltpu.get_barrier_semaphore()

    def greet(j, carry):
        pl.semaphore_signal(barrier, inc=1, device_id=to_patch(patch_peer(j)), device_id_type=MESH)
        pl.semaphore_signal(barrier, inc=1, device_id=to_tm(tm_peer(j)), device_id_type=MESH)
        return carry

    lax.fori_loop(1, N, greet, 0)

    loads = []
    for half in range(2):
        for a, ref in enumerate((q_hbm, k_hbm, v_hbm, g_hbm)):
            cols = pl.ds(half * 512, 512)
            copy = pltpu.make_async_copy(
                ref.at[0, :, :, cols], inp.at[a, :, :, cols], in_sem.at[half, a]
            )
            copy.start()
            loads.append(copy)

    ws_copy = pltpu.make_async_copy(ws_hbm, ws_ref, ws_sem)
    ws_copy.start()

    def pack_spatial(c, d):
        f = d // 4
        cols = pl.ds(pl.multiple_of((d % 4) * 128, 128), 128)
        q, k, v, g = (inp[a, f, :, cols] for a in range(4))
        h = slice(c * 64, c * 64 + 64)
        return (
            jnp.concatenate([q[:, h], g[:, h]], axis=1),
            jnp.concatenate([k[:, h], v[:, h]], axis=1),
        )

    own_rows = pl.ds(pl.multiple_of(me_p * PT, PT), PT)

    def s_copy(c, d):
        return pltpu.make_async_remote_copy(
            src_ref=s_send.at[d, c],
            dst_ref=s_in.at[c, :, own_rows, :],
            send_sem=ss_sem.at[c],
            recv_sem=sr_sem.at[c],
            device_id=to_patch(d),
            device_id_type=MESH,
        )

    def s_all(c):
        return pltpu.make_async_remote_copy(
            src_ref=s_send.at[pl.ds(0, N - 1), c],
            dst_ref=s_in.at[c, :, pl.ds(0, (N - 1) * PT), :],
            send_sem=ss_sem.at[c],
            recv_sem=sr_sem.at[c],
            device_id=to_patch(patch_peer(1)),
            device_id_type=MESH,
        )

    def t_copy(e):
        return pltpu.make_async_remote_copy(
            src_ref=t_send.at[0, e],
            dst_ref=t_in.at[me_t],
            send_sem=ts_sem,
            recv_sem=tr_sem,
            device_id=to_tm(e),
            device_id_type=MESH,
        )

    def t_all():
        return pltpu.make_async_remote_copy(
            src_ref=t_send.at[0, pl.ds(0, N - 1)],
            dst_ref=t_in.at[pl.ds(0, N - 1)],
            send_sem=ts_sem,
            recv_sem=tr_sem,
            device_id=to_tm(tm_peer(1)),
            device_id_type=MESH,
        )

    def b_copy(c, d):
        return pltpu.make_async_remote_copy(
            src_ref=s_out.at[c, :, pl.ds(pl.multiple_of(d * PT, PT), PT), :],
            dst_ref=s_back.at[me_p, c],
            send_sem=bs_sem.at[c],
            recv_sem=br_sem.at[me_p] if c else b0_sem,
            device_id=to_patch(d),
            device_id_type=MESH,
        )

    def b_arrival(d):
        return pltpu.make_async_remote_copy(
            src_ref=s_out.at[1, :, pl.ds(pl.multiple_of(d * PT, PT), PT), :],
            dst_ref=s_back.at[d, 1],
            send_sem=bs_sem.at[1],
            recv_sem=br_sem.at[d],
            device_id=to_patch(d),
            device_id_type=MESH,
        )

    def b_all(c):
        return pltpu.make_async_remote_copy(
            src_ref=s_out.at[c, :, pl.ds(0, (N - 1) * PT), :],
            dst_ref=s_back.at[pl.ds(0, N - 1), c],
            send_sem=bs_sem.at[c],
            recv_sem=b0_sem,
            device_id=to_patch(patch_peer(1)),
            device_id_type=MESH,
        )

    def u_copy(e):
        return pltpu.make_async_remote_copy(
            src_ref=t_send.at[1, e],
            dst_ref=t_back.at[me_t],
            send_sem=us_sem,
            recv_sem=ur_sem,
            device_id=to_tm(e),
            device_id_type=MESH,
        )

    def u_all():
        return pltpu.make_async_remote_copy(
            src_ref=t_send.at[1, pl.ds(0, N - 1)],
            dst_ref=t_back.at[pl.ds(0, N - 1)],
            send_sem=us_sem,
            recv_sem=ur_sem,
            device_id=to_tm(tm_peer(1)),
            device_id_type=MESH,
        )

    def each(peer, act):
        def body(j, carry):
            act(peer(j))
            return carry

        lax.fori_loop(1, N, body, 0)

    for copy in loads[:4]:
        copy.wait()
    pl.semaphore_wait(barrier, 2 * (N - 1))

    def send_spatial(c, d):
        parts = pack_spatial(c, d)
        for s in range(2):
            s_send[d, c, s] = parts[s]
        s_copy(c, d).start()

    for copy in loads[4:]:
        copy.wait()

    def pack_temporal(e):
        rows = pl.ds(pl.multiple_of((e // 4) * 16, 16), 16)
        cols = pl.ds(pl.multiple_of(512 + (e % 4) * 128, 128), 128)
        return [inp[a, :, rows, cols] for a in range(4)]

    def send_temporal(e):
        parts = pack_temporal(e)
        for a in range(4):
            t_send[0, e, a] = parts[a]
        t_copy(e).start()

    def both(j, carry):
        send_spatial(0, patch_peer(j))
        send_temporal(tm_peer(j))
        return carry

    lax.fori_loop(1, N, both, 0)
    each(patch_peer, lambda d: send_spatial(1, d))
    for c in range(2):
        parts = pack_spatial(c, me_p)
        for s in range(2):
            s_in[c, s, own_rows, :] = parts[s]
    parts = pack_temporal(me_t)
    for a in range(4):
        t_in[me_t, a] = parts[a]

    def spatial(c):
        s_all(c).wait_recv()
        low = lax.broadcasted_iota(jnp.int32, (QB, 128), 1) < 64

        def turn(i, carry):
            rows = pl.ds(pl.multiple_of(i * QB, QB), QB)
            a = s_in[c, 0, rows, :].astype(F32)
            tr_a[:, rows] = jnp.where(low, a * SCALE, a).T.astype(BF16)
            return carry

        lax.fori_loop(0, 1024 // QB, turn, 0)
        acc[...] = jnp.zeros_like(acc)

        def block(i, carry):
            rows = pl.ds(pl.multiple_of(i * QB, QB), QB)
            a = s_in[c, 0, rows, :]
            b = s_in[c, 1]
            zero = jnp.zeros_like(a)
            a_q = jnp.where(low, a * SCALE, zero)
            a_g = jnp.where(low, zero, a)
            scores = dot(a_q, b, 1, 1)
            weight_grad = dot(a_g, b, 1, 1)
            e = jnp.exp(scores - jnp.max(scores, axis=1, keepdims=True))
            w = e * (1.0 / jnp.sum(e, axis=1, keepdims=True))
            delta = jnp.sum(w * weight_grad, axis=1, keepdims=True)
            ds_b = (w * (weight_grad - delta)).astype(BF16)
            w_b = w.astype(BF16)
            out = jnp.where(low, dot(ds_b, b, 1, 0) * SCALE, dot(w_b, b, 1, 0))
            s_out[c, 0, rows, :] = out.astype(BF16)
            acc[0:64, :] += dot(tr_a[0:64, rows], ds_b, 1, 0)
            acc[64:128, :] += dot(tr_a[64:128, rows], w_b, 1, 0)
            return carry

        lax.fori_loop(0, 1024 // QB, block, 0)

        def back(i, carry):
            rows = pl.ds(pl.multiple_of(i * QB, QB), QB)
            s_out[c, 1, rows, :] = acc[:, rows].T.astype(BF16)
            return carry

        lax.fori_loop(0, 1024 // QB, back, 0)
        def first(d, carry):
            @pl.when(d != me_p)
            def _():
                b_copy(c, d).start()

            return carry

        def later(j, carry):
            d = patch_peer(j)

            @pl.when(d >= 4)
            def _():
                b_copy(c, d).start()

            return carry

        lax.fori_loop(0, 4, first, 0)
        lax.fori_loop(1, N, later, 0)
        for s in range(2):
            s_back[me_p, c, s] = s_out[c, s, own_rows, :]

    def temporal():
        ws_copy.wait()
        t_all().wait_recv()

        def widen(e, carry):
            for a in range(4):
                rows = pl.ds(pl.multiple_of(e * 64, 64), 64)
                t_f32[a, rows, :] = t_in[e, a].reshape(64, 128).astype(F32)
            return carry

        lax.fori_loop(0, N, widen, 0)
        i0 = lax.broadcasted_iota(jnp.int32, (64, 64), 0)
        i1 = lax.broadcasted_iota(jnp.int32, (64, 64), 1)
        starts = jnp.sum(
            jnp.where(i0 == i1, jnp.broadcast_to(ws_ref[...].astype(F32), (64, 64)), 0.0),
            axis=1, keepdims=True,
        )
        lanes = lax.broadcasted_iota(jnp.int32, (64, 128), 1)
        low = lanes < 64
        frame = jnp.where(low, lanes, lanes - 64).astype(F32)
        allowed = (frame >= starts) & (frame < starts + WINDOW)
        allowed_0 = allowed & low
        allowed_1 = allowed & ~low

        def halves(x, op, fill, mask_0, mask_1):
            r0 = op(jnp.where(mask_0, x, fill), axis=1, keepdims=True)
            r1 = op(jnp.where(mask_1, x, fill), axis=1, keepdims=True)
            return jnp.where(low, r0, r1)

        def diagonal(x):
            return jnp.concatenate(
                [jnp.where(low, x, 0.0), jnp.where(low, 0.0, x)], axis=0
            ).astype(BF16)

        def patches(i, carry):
            group = [pl.ds(i * GROUP + u, 64, stride=16) for u in range(GROUP)]
            items = []
            for rows in group:
                q, k, v, g = (t_f32[a, rows, :] for a in range(4))
                items.append(((q * SCALE).astype(BF16), diagonal(k), diagonal(v), g.astype(BF16)))
            scores = [dot(q, k_d, 1, 1) for q, k_d, v_d, g in items]
            weight_grads = [dot(g, v_d, 1, 1) for q, k_d, v_d, g in items]
            highest = [halves(x, jnp.max, -1e30, allowed_0, allowed_1) for x in scores]
            exps = [
                jnp.where(allowed, jnp.exp(x - m), 0.0) for x, m in zip(scores, highest)
            ]
            ws = [e * (1.0 / halves(e, jnp.sum, 0.0, low, ~low)) for e in exps]
            deltas = [
                halves(w * x, jnp.sum, 0.0, low, ~low) for w, x in zip(ws, weight_grads)
            ]
            grads = [
                (w * (x - m)).astype(BF16) for w, x, m in zip(ws, weight_grads, deltas)
            ]
            ws = [w.astype(BF16) for w in ws]
            for rows, (q, k_d, v_d, g), w_b, ds_b in zip(group, items, ws, grads):
                dk = dot(ds_b, q, 0, 0)
                dv = dot(w_b, g, 0, 0)
                t_res[0, rows, :] = dot(w_b, v_d, 1, 0)
                t_res[1, rows, :] = dot(ds_b, k_d, 1, 0) * SCALE
                t_res[2, rows, :] = jnp.where(low, dk[:64], dk[64:])
                t_res[3, rows, :] = jnp.where(low, dv[:64], dv[64:])
            return carry

        lax.fori_loop(0, 16 // GROUP, patches, 0)

        def narrow(e):
            rows = pl.ds(pl.multiple_of(e * 64, 64), 64)
            return [t_res[a, rows, :].astype(BF16).reshape(4, 16, 128) for a in range(4)]

        def send_back(e):
            parts = narrow(e)
            for a in range(4):
                t_send[1, e, a] = parts[a]
            u_copy(e).start()

        each(tm_peer, send_back)
        parts = narrow(me_t)
        for a in range(4):
            t_back[me_t, a] = parts[a]

    spatial(0)
    temporal()
    spatial(1)

    outs = (o_ref, dq_ref, dk_ref, dv_ref)

    def unpack_temporal(e):
        rows = pl.ds(pl.multiple_of((e // 4) * 16, 16), 16)
        cols = pl.ds(pl.multiple_of(512 + (e % 4) * 128, 128), 128)
        for a in range(4):
            outs[a][0, :, rows, cols] = t_back[e, a]

    u_all().wait_recv()
    unpack_temporal(me_t)
    each(tm_peer, unpack_temporal)

    def unpack_spatial(d):
        f = d // 4
        cols = pl.ds(pl.multiple_of((d % 4) * 128, 128), 128)
        for s, (low_ref, high_ref) in enumerate(((dq_ref, o_ref), (dk_ref, dv_ref))):
            x, y = s_back[d, 0, s], s_back[d, 1, s]
            low_ref[0, f, :, cols] = jnp.concatenate([x[:, :64], y[:, :64]], axis=1)
            high_ref[0, f, :, cols] = jnp.concatenate([x[:, 64:], y[:, 64:]], axis=1)

    unpack_spatial(me_p)
    t_all().wait_send()
    u_all().wait_send()
    for c in range(2):
        s_all(c).wait_send()
    b_all(0).wait()

    def take_spatial(d):
        b_arrival(d).wait_recv()
        unpack_spatial(d)

    each(patch_peer, take_spatial)
    b_all(1).wait_send()


def emit(*refs):
    sem = refs[8]
    copies = [
        pltpu.make_async_copy(src, dst, sem.at[a])
        for a, (src, dst) in enumerate(zip(refs[:4], refs[4:8]))
    ]
    for copy in copies:
        copy.start()
    for copy in copies:
        copy.wait()


def on_device(queries, key_vectors, value_vectors, grad_output, window_start):
    anywhere = pl.BlockSpec(memory_space=pltpu.HBM)
    vmem = pl.BlockSpec(memory_space=pltpu.VMEM)
    dma = pltpu.SemaphoreType.DMA
    shape = jax.ShapeDtypeStruct((1, FR, PT, 1024), BF16)
    results = pl.pallas_call(
        kernel,
        out_shape=(shape,) * 4,
        in_specs=[anywhere] * 5,
        out_specs=(vmem,) * 4,
        scratch_shapes=[
            pltpu.VMEM((1, 64), jnp.int32),
            pltpu.VMEM((4, FR, PT, 1024), BF16),
            pltpu.VMEM((N, 2, 2, PT, 128), BF16),
            pltpu.VMEM((2, N, 4, FR, 16, 128), BF16),
            pltpu.VMEM((2, 2, 1024, 128), BF16),
            pltpu.VMEM((N, 4, FR, 16, 128), BF16),
            pltpu.VMEM((4, 1024, 128), F32),
            pltpu.VMEM((4, 1024, 128), F32),
            pltpu.VMEM((128, 1024), BF16),
            pltpu.VMEM((128, 1024), F32),
            pltpu.VMEM((2, 2, 1024, 128), BF16),
            pltpu.VMEM((N, 2, 2, PT, 128), BF16),
            pltpu.VMEM((N, 4, FR, 16, 128), BF16),
            dma, dma((2, 4)),
            dma((2,)), dma((2,)), dma, dma, dma((2,)), dma, dma((N,)), dma, dma,
        ],
        compiler_params=pltpu.CompilerParams(
            collective_id=0, has_side_effects=True, vmem_limit_bytes=52900 << 10
        ),
        name="attention",
    )(queries, key_vectors, value_vectors, grad_output, window_start.reshape(1, 64))
    return pl.pallas_call(
        emit,
        out_shape=(shape,) * 4,
        in_specs=[vmem] * 4,
        out_specs=(anywhere,) * 4,
        scratch_shapes=[dma((4,))],
        compiler_params=pltpu.CompilerParams(vmem_limit_bytes=6 << 20),
        name="emit",
    )(*results)


def solution(mesh):
    spec = P(None, "tm", "patch", None)
    return jax.shard_map(
        on_device,
        mesh=mesh,
        in_specs=(spec,) * 4 + (P(),),
        out_specs=(spec,) * 4,
        check_vma=False,
    )
```

```python
import functools

import jax
import jax.numpy as jnp
from jax import lax
from jax.experimental import pallas as pl
from jax.experimental.pallas import tpu as pltpu
from jax.sharding import PartitionSpec as P

MESH = pl.DeviceIdType.MESH
BF16 = jnp.bfloat16
F32 = jnp.float32
N = 16
FR = 4
PT = 64
WINDOW = 16
SCALE = 0.125
GROUP = 8
QB = 256


def dot(a, b, ca, cb):
    return lax.dot_general(a, b, (((ca,), (cb,)), ((), ())), preferred_element_type=F32)


def kernel(
    q_hbm, k_hbm, v_hbm, g_hbm, ws_hbm,
    o_ref, dq_ref, dk_ref, dv_ref,
    ws_ref, inp, s_send, t_send, s_in, t_in, t_f32, t_res, tr_a, acc, s_out, s_back, t_back,
    ws_sem, in_sem, ss_sem, sr_sem, ts_sem, tr_sem, bs_sem, b0_sem, br_sem, us_sem, ur_sem,
):
    me_t = lax.axis_index("tm")
    me_p = lax.axis_index("patch")

    def patch_peer(j):
        z = (me_p // 2 + j // 2) % 8
        y = (me_p % 2 + j % 2) % 2
        return z * 2 + y

    def tm_peer(j):
        return (me_t + j) % N

    def to_patch(d):
        return (me_t, d)

    def to_tm(e):
        return (e, me_p)

    barrier = pltpu.get_barrier_semaphore()

    def greet(j, carry):
        pl.semaphore_signal(barrier, inc=1, device_id=to_patch(patch_peer(j)), device_id_type=MESH)
        pl.semaphore_signal(barrier, inc=1, device_id=to_tm(tm_peer(j)), device_id_type=MESH)
        return carry

    lax.fori_loop(1, N, greet, 0)

    for half in range(2):
        for a, ref in enumerate((q_hbm, k_hbm, v_hbm, g_hbm)):
            cols = pl.ds(half * 512, 512)
            copy = pltpu.make_async_copy(
                ref.at[0, :, :, cols], inp.at[a, :, :, cols], in_sem.at[half]
            )
            copy.start()

    def half_loaded(half):
        cols = inp.at[:, :, :, pl.ds(half * 512, 512)]
        return pltpu.make_async_copy(cols, cols, in_sem.at[half])

    ws_copy = pltpu.make_async_copy(ws_hbm, ws_ref, ws_sem)
    ws_copy.start()

    def pack_spatial(c, d):
        f = d // 4
        cols = pl.ds(pl.multiple_of((d % 4) * 128, 128), 128)
        q, k, v, g = (inp[a, f, :, cols] for a in range(4))
        h = slice(c * 64, c * 64 + 64)
        return (
            jnp.concatenate([q[:, h], g[:, h]], axis=1),
            jnp.concatenate([k[:, h], v[:, h]], axis=1),
        )

    own_rows = pl.ds(pl.multiple_of(me_p * PT, PT), PT)

    def s_copy(c, d):
        return pltpu.make_async_remote_copy(
            src_ref=s_send.at[d, c],
            dst_ref=s_in.at[c, :, own_rows, :],
            send_sem=ss_sem.at[c],
            recv_sem=sr_sem.at[c],
            device_id=to_patch(d),
            device_id_type=MESH,
        )

    def s_all(c):
        return pltpu.make_async_remote_copy(
            src_ref=s_send.at[pl.ds(0, N - 1), c],
            dst_ref=s_in.at[c, :, pl.ds(0, (N - 1) * PT), :],
            send_sem=ss_sem.at[c],
            recv_sem=sr_sem.at[c],
            device_id=to_patch(patch_peer(1)),
            device_id_type=MESH,
        )

    def t_copy(e):
        return pltpu.make_async_remote_copy(
            src_ref=t_send.at[0, e],
            dst_ref=t_in.at[me_t],
            send_sem=ts_sem,
            recv_sem=tr_sem,
            device_id=to_tm(e),
            device_id_type=MESH,
        )

    def t_all():
        return pltpu.make_async_remote_copy(
            src_ref=t_send.at[0, pl.ds(0, N - 1)],
            dst_ref=t_in.at[pl.ds(0, N - 1)],
            send_sem=ts_sem,
            recv_sem=tr_sem,
            device_id=to_tm(tm_peer(1)),
            device_id_type=MESH,
        )

    def b_copy(c, d):
        return pltpu.make_async_remote_copy(
            src_ref=s_out.at[c, :, pl.ds(pl.multiple_of(d * PT, PT), PT), :],
            dst_ref=s_back.at[me_p, c],
            send_sem=bs_sem.at[c],
            recv_sem=br_sem.at[me_p] if c else b0_sem,
            device_id=to_patch(d),
            device_id_type=MESH,
        )

    def b_arrival(d):
        return pltpu.make_async_remote_copy(
            src_ref=s_out.at[1, :, pl.ds(pl.multiple_of(d * PT, PT), PT), :],
            dst_ref=s_back.at[d, 1],
            send_sem=bs_sem.at[1],
            recv_sem=br_sem.at[d],
            device_id=to_patch(d),
            device_id_type=MESH,
        )

    def b_all(c):
        return pltpu.make_async_remote_copy(
            src_ref=s_out.at[c, :, pl.ds(0, (N - 1) * PT), :],
            dst_ref=s_back.at[pl.ds(0, N - 1), c],
            send_sem=bs_sem.at[c],
            recv_sem=b0_sem,
            device_id=to_patch(patch_peer(1)),
            device_id_type=MESH,
        )

    def u_copy(e):
        return pltpu.make_async_remote_copy(
            src_ref=t_send.at[1, e],
            dst_ref=t_back.at[me_t],
            send_sem=us_sem,
            recv_sem=ur_sem,
            device_id=to_tm(e),
            device_id_type=MESH,
        )

    def u_all():
        return pltpu.make_async_remote_copy(
            src_ref=t_send.at[1, pl.ds(0, N - 1)],
            dst_ref=t_back.at[pl.ds(0, N - 1)],
            send_sem=us_sem,
            recv_sem=ur_sem,
            device_id=to_tm(tm_peer(1)),
            device_id_type=MESH,
        )

    def each(peer, act):
        def body(j, carry):
            act(peer(j))
            return carry

        lax.fori_loop(1, N, body, 0)

    half_loaded(0).wait()
    pl.semaphore_wait(barrier, 2 * (N - 1))

    def send_spatial(c, d):
        parts = pack_spatial(c, d)
        for s in range(2):
            s_send[d, c, s] = parts[s]
        s_copy(c, d).start()

    half_loaded(1).wait()

    def pack_temporal(e):
        rows = pl.ds(pl.multiple_of((e // 4) * 16, 16), 16)
        cols = pl.ds(pl.multiple_of(512 + (e % 4) * 128, 128), 128)
        return [inp[a, :, rows, cols] for a in range(4)]

    def send_temporal(e):
        parts = pack_temporal(e)
        for a in range(4):
            t_send[0, e, a] = parts[a]
        t_copy(e).start()

    def both(j, carry):
        send_spatial(0, patch_peer(j))
        send_temporal(tm_peer(j))
        return carry

    lax.fori_loop(1, N, both, 0)
    each(patch_peer, lambda d: send_spatial(1, d))
    for c in range(2):
        parts = pack_spatial(c, me_p)
        for s in range(2):
            s_in[c, s, own_rows, :] = parts[s]
    parts = pack_temporal(me_t)
    for a in range(4):
        t_in[me_t, a] = parts[a]

    def spatial(c):
        s_all(c).wait_recv()
        low = lax.broadcasted_iota(jnp.int32, (QB, 128), 1) < 64

        def turn(i, carry):
            rows = pl.ds(pl.multiple_of(i * QB, QB), QB)
            a = s_in[c, 0, rows, :].astype(F32)
            tr_a[:, rows] = jnp.where(low, a * SCALE, a).T.astype(BF16)
            return carry

        lax.fori_loop(0, 1024 // QB, turn, 0)
        acc[...] = jnp.zeros_like(acc)

        def block(i, carry):
            rows = pl.ds(pl.multiple_of(i * QB, QB), QB)
            a = s_in[c, 0, rows, :]
            b = s_in[c, 1]
            zero = jnp.zeros_like(a)
            a_q = jnp.where(low, a * SCALE, zero)
            a_g = jnp.where(low, zero, a)
            scores = dot(a_q, b, 1, 1)
            weight_grad = dot(a_g, b, 1, 1)
            e = jnp.exp(scores - jnp.max(scores, axis=1, keepdims=True))
            w = e * (1.0 / jnp.sum(e, axis=1, keepdims=True))
            delta = jnp.sum(w * weight_grad, axis=1, keepdims=True)
            ds_b = (w * (weight_grad - delta)).astype(BF16)
            w_b = w.astype(BF16)
            out = jnp.where(low, dot(ds_b, b, 1, 0) * SCALE, dot(w_b, b, 1, 0))
            s_out[c, 0, rows, :] = out.astype(BF16)
            acc[0:64, :] += dot(tr_a[0:64, rows], ds_b, 1, 0)
            acc[64:128, :] += dot(tr_a[64:128, rows], w_b, 1, 0)
            return carry

        lax.fori_loop(0, 1024 // QB, block, 0)

        def back(i, carry):
            rows = pl.ds(pl.multiple_of(i * QB, QB), QB)
            s_out[c, 1, rows, :] = acc[:, rows].T.astype(BF16)
            return carry

        lax.fori_loop(0, 1024 // QB, back, 0)
        def first(d, carry):
            @pl.when(d != me_p)
            def _():
                b_copy(c, d).start()

            return carry

        def later(j, carry):
            d = patch_peer(j)

            @pl.when(d >= 4)
            def _():
                b_copy(c, d).start()

            return carry

        lax.fori_loop(0, 4, first, 0)
        lax.fori_loop(1, N, later, 0)
        for s in range(2):
            s_back[me_p, c, s] = s_out[c, s, own_rows, :]

    def temporal():
        ws_copy.wait()
        t_all().wait_recv()

        def widen(e, carry):
            for a in range(4):
                rows = pl.ds(pl.multiple_of(e * 64, 64), 64)
                t_f32[a, rows, :] = t_in[e, a].reshape(64, 128).astype(F32)
            return carry

        lax.fori_loop(0, N, widen, 0)
        i0 = lax.broadcasted_iota(jnp.int32, (64, 64), 0)
        i1 = lax.broadcasted_iota(jnp.int32, (64, 64), 1)
        starts = jnp.sum(
            jnp.where(i0 == i1, jnp.broadcast_to(ws_ref[...].astype(F32), (64, 64)), 0.0),
            axis=1, keepdims=True,
        )
        lanes = lax.broadcasted_iota(jnp.int32, (64, 128), 1)
        low = lanes < 64
        frame = jnp.where(low, lanes, lanes - 64).astype(F32)
        allowed = (frame >= starts) & (frame < starts + WINDOW)
        allowed_0 = allowed & low
        allowed_1 = allowed & ~low

        def halves(x, op, fill, mask_0, mask_1):
            r0 = op(jnp.where(mask_0, x, fill), axis=1, keepdims=True)
            r1 = op(jnp.where(mask_1, x, fill), axis=1, keepdims=True)
            return jnp.where(low, r0, r1)

        def diagonal(x):
            return jnp.concatenate(
                [jnp.where(low, x, 0.0), jnp.where(low, 0.0, x)], axis=0
            ).astype(BF16)

        def patches(i, carry):
            group = [pl.ds(i * GROUP + u, 64, stride=16) for u in range(GROUP)]
            items = []
            for rows in group:
                q, k, v, g = (t_f32[a, rows, :] for a in range(4))
                items.append(((q * SCALE).astype(BF16), diagonal(k), diagonal(v), g.astype(BF16)))
            scores = [dot(q, k_d, 1, 1) for q, k_d, v_d, g in items]
            weight_grads = [dot(g, v_d, 1, 1) for q, k_d, v_d, g in items]
            highest = [halves(x, jnp.max, -1e30, allowed_0, allowed_1) for x in scores]
            exps = [
                jnp.where(allowed, jnp.exp(x - m), 0.0) for x, m in zip(scores, highest)
            ]
            ws = [e * (1.0 / halves(e, jnp.sum, 0.0, low, ~low)) for e in exps]
            deltas = [
                halves(w * x, jnp.sum, 0.0, low, ~low) for w, x in zip(ws, weight_grads)
            ]
            grads = [
                (w * (x - m)).astype(BF16) for w, x, m in zip(ws, weight_grads, deltas)
            ]
            ws = [w.astype(BF16) for w in ws]
            for rows, (q, k_d, v_d, g), w_b, ds_b in zip(group, items, ws, grads):
                dk = dot(ds_b, q, 0, 0)
                dv = dot(w_b, g, 0, 0)
                t_res[0, rows, :] = dot(w_b, v_d, 1, 0)
                t_res[1, rows, :] = dot(ds_b, k_d, 1, 0) * SCALE
                t_res[2, rows, :] = jnp.where(low, dk[:64], dk[64:])
                t_res[3, rows, :] = jnp.where(low, dv[:64], dv[64:])
            return carry

        lax.fori_loop(0, 16 // GROUP, patches, 0)

        def narrow(e):
            rows = pl.ds(pl.multiple_of(e * 64, 64), 64)
            return [t_res[a, rows, :].astype(BF16).reshape(4, 16, 128) for a in range(4)]

        def send_back(e):
            parts = narrow(e)
            for a in range(4):
                t_send[1, e, a] = parts[a]
            u_copy(e).start()

        each(tm_peer, send_back)
        parts = narrow(me_t)
        for a in range(4):
            t_back[me_t, a] = parts[a]

    spatial(0)
    temporal()
    spatial(1)

    outs = (o_ref, dq_ref, dk_ref, dv_ref)

    def unpack_temporal(e):
        rows = pl.ds(pl.multiple_of((e // 4) * 16, 16), 16)
        cols = pl.ds(pl.multiple_of(512 + (e % 4) * 128, 128), 128)
        for a in range(4):
            outs[a][0, :, rows, cols] = t_back[e, a]

    u_all().wait_recv()
    unpack_temporal(me_t)
    each(tm_peer, unpack_temporal)

    def unpack_spatial(d):
        f = d // 4
        cols = pl.ds(pl.multiple_of((d % 4) * 128, 128), 128)
        for s, (low_ref, high_ref) in enumerate(((dq_ref, o_ref), (dk_ref, dv_ref))):
            x, y = s_back[d, 0, s], s_back[d, 1, s]
            low_ref[0, f, :, cols] = jnp.concatenate([x[:, :64], y[:, :64]], axis=1)
            high_ref[0, f, :, cols] = jnp.concatenate([x[:, 64:], y[:, 64:]], axis=1)

    unpack_spatial(me_p)
    t_all().wait_send()
    u_all().wait_send()
    for c in range(2):
        s_all(c).wait_send()
    b_all(0).wait()

    def take_spatial(d):
        b_arrival(d).wait_recv()
        unpack_spatial(d)

    each(patch_peer, take_spatial)
    b_all(1).wait_send()


def emit(*refs):
    sem = refs[8]
    copies = [
        pltpu.make_async_copy(src, dst, sem.at[a])
        for a, (src, dst) in enumerate(zip(refs[:4], refs[4:8]))
    ]
    for copy in copies:
        copy.start()
    for copy in copies:
        copy.wait()


def on_device(queries, key_vectors, value_vectors, grad_output, window_start):
    anywhere = pl.BlockSpec(memory_space=pltpu.HBM)
    vmem = pl.BlockSpec(memory_space=pltpu.VMEM)
    dma = pltpu.SemaphoreType.DMA
    shape = jax.ShapeDtypeStruct((1, FR, PT, 1024), BF16)
    inputs = (queries, key_vectors, value_vectors, grad_output, window_start.reshape(1, 64))
    results = pl.pallas_call(
        kernel,
        out_shape=(shape,) * 4,
        in_specs=[anywhere] * 5,
        out_specs=(vmem,) * 4,
        scratch_shapes=[
            pltpu.VMEM((1, 64), jnp.int32),
            pltpu.VMEM((4, FR, PT, 1024), BF16),
            pltpu.VMEM((N, 2, 2, PT, 128), BF16),
            pltpu.VMEM((2, N, 4, FR, 16, 128), BF16),
            pltpu.VMEM((2, 2, 1024, 128), BF16),
            pltpu.VMEM((N, 4, FR, 16, 128), BF16),
            pltpu.VMEM((4, 1024, 128), F32),
            pltpu.VMEM((4, 1024, 128), F32),
            pltpu.VMEM((128, 1024), BF16),
            pltpu.VMEM((128, 1024), F32),
            pltpu.VMEM((2, 2, 1024, 128), BF16),
            pltpu.VMEM((N, 2, 2, PT, 128), BF16),
            pltpu.VMEM((N, 4, FR, 16, 128), BF16),
            dma, dma((2,)),
            dma((2,)), dma((2,)), dma, dma, dma((2,)), dma, dma((N,)), dma, dma,
        ],
        compiler_params=pltpu.CompilerParams(
            collective_id=0, has_side_effects=True, vmem_limit_bytes=48 << 20
        ),
        name="attention",
    )(*(pltpu.with_memory_space_constraint(x, pltpu.HBM) for x in inputs))
    return pl.pallas_call(
        emit,
        out_shape=(shape,) * 4,
        in_specs=[vmem] * 4,
        out_specs=(anywhere,) * 4,
        scratch_shapes=[dma((4,))],
        compiler_params=pltpu.CompilerParams(vmem_limit_bytes=6 << 20),
        name="emit",
    )(*(pltpu.with_memory_space_constraint(x, pltpu.VMEM) for x in results))


def solution(mesh):
    spec = P(None, "tm", "patch", None)
    return jax.shard_map(
        on_device,
        mesh=mesh,
        in_specs=(spec,) * 4 + (P(),),
        out_specs=(spec,) * 4,
        check_vma=False,
    )
```

```python
import functools

import jax
import jax.numpy as jnp
from jax import lax
from jax.experimental import pallas as pl
from jax.experimental.pallas import tpu as pltpu
from jax.sharding import PartitionSpec as P

MESH = pl.DeviceIdType.MESH
BF16 = jnp.bfloat16
F32 = jnp.float32
N = 16
FR = 4
PT = 64
WINDOW = 16
SCALE = 0.125
GROUP = 8
QB = 512


def dot(a, b, ca, cb):
    return lax.dot_general(a, b, (((ca,), (cb,)), ((), ())), preferred_element_type=F32)


def kernel(
    q_hbm, k_hbm, v_hbm, g_hbm, ws_hbm,
    o_ref, dq_ref, dk_ref, dv_ref,
    ws_ref, inp, s_send, t_send, s_in, t_in, t_f32, t_res, tr_a, acc, s_out, s_back, t_back,
    ws_sem, in_sem, ss_sem, sr_sem, ts_sem, tr_sem, bs_sem, b0_sem, br_sem, us_sem, ur_sem,
):
    me_t = lax.axis_index("tm")
    me_p = lax.axis_index("patch")

    def patch_peer(j):
        z = (me_p // 2 + j // 2) % 8
        y = (me_p % 2 + j % 2) % 2
        return z * 2 + y

    def tm_peer(j):
        return (me_t + j) % N

    def to_patch(d):
        return (me_t, d)

    def to_tm(e):
        return (e, me_p)

    barrier = pltpu.get_barrier_semaphore()

    def greet(j, carry):
        pl.semaphore_signal(barrier, inc=1, device_id=to_patch(patch_peer(j)), device_id_type=MESH)
        pl.semaphore_signal(barrier, inc=1, device_id=to_tm(tm_peer(j)), device_id_type=MESH)
        return carry

    lax.fori_loop(1, N, greet, 0)

    for half in range(2):
        for a, ref in enumerate((q_hbm, k_hbm, v_hbm, g_hbm)):
            cols = pl.ds(half * 512, 512)
            copy = pltpu.make_async_copy(
                ref.at[0, :, :, cols], inp.at[a, :, :, cols], in_sem.at[half]
            )
            copy.start()

    def half_loaded(half):
        cols = inp.at[:, :, :, pl.ds(half * 512, 512)]
        return pltpu.make_async_copy(cols, cols, in_sem.at[half])

    ws_copy = pltpu.make_async_copy(ws_hbm, ws_ref, ws_sem)
    ws_copy.start()

    def pack_spatial(c, d):
        f = d // 4
        cols = pl.ds(pl.multiple_of((d % 4) * 128, 128), 128)
        q, k, v, g = (inp[a, f, :, cols] for a in range(4))
        h = slice(c * 64, c * 64 + 64)
        return (
            jnp.concatenate([q[:, h], g[:, h]], axis=1),
            jnp.concatenate([k[:, h], v[:, h]], axis=1),
        )

    own_rows = pl.ds(pl.multiple_of(me_p * PT, PT), PT)

    def s_copy(c, d):
        return pltpu.make_async_remote_copy(
            src_ref=s_send.at[d, c],
            dst_ref=s_in.at[c, :, own_rows, :],
            send_sem=ss_sem.at[c],
            recv_sem=sr_sem.at[c],
            device_id=to_patch(d),
            device_id_type=MESH,
        )

    def s_all(c):
        return pltpu.make_async_remote_copy(
            src_ref=s_send.at[pl.ds(0, N - 1), c],
            dst_ref=s_in.at[c, :, pl.ds(0, (N - 1) * PT), :],
            send_sem=ss_sem.at[c],
            recv_sem=sr_sem.at[c],
            device_id=to_patch(patch_peer(1)),
            device_id_type=MESH,
        )

    def t_copy(e):
        return pltpu.make_async_remote_copy(
            src_ref=t_send.at[0, e],
            dst_ref=t_in.at[me_t],
            send_sem=ts_sem,
            recv_sem=tr_sem,
            device_id=to_tm(e),
            device_id_type=MESH,
        )

    def t_all():
        return pltpu.make_async_remote_copy(
            src_ref=t_send.at[0, pl.ds(0, N - 1)],
            dst_ref=t_in.at[pl.ds(0, N - 1)],
            send_sem=ts_sem,
            recv_sem=tr_sem,
            device_id=to_tm(tm_peer(1)),
            device_id_type=MESH,
        )

    def b_copy(c, d):
        return pltpu.make_async_remote_copy(
            src_ref=s_out.at[c, :, pl.ds(pl.multiple_of(d * PT, PT), PT), :],
            dst_ref=s_back.at[me_p, c],
            send_sem=bs_sem.at[c],
            recv_sem=br_sem.at[me_p] if c else b0_sem,
            device_id=to_patch(d),
            device_id_type=MESH,
        )

    def b_arrival(d):
        return pltpu.make_async_remote_copy(
            src_ref=s_out.at[1, :, pl.ds(pl.multiple_of(d * PT, PT), PT), :],
            dst_ref=s_back.at[d, 1],
            send_sem=bs_sem.at[1],
            recv_sem=br_sem.at[d],
            device_id=to_patch(d),
            device_id_type=MESH,
        )

    def b_all(c):
        return pltpu.make_async_remote_copy(
            src_ref=s_out.at[c, :, pl.ds(0, (N - 1) * PT), :],
            dst_ref=s_back.at[pl.ds(0, N - 1), c],
            send_sem=bs_sem.at[c],
            recv_sem=b0_sem,
            device_id=to_patch(patch_peer(1)),
            device_id_type=MESH,
        )

    def u_copy(e):
        return pltpu.make_async_remote_copy(
            src_ref=t_send.at[1, e],
            dst_ref=t_back.at[me_t],
            send_sem=us_sem,
            recv_sem=ur_sem,
            device_id=to_tm(e),
            device_id_type=MESH,
        )

    def u_all():
        return pltpu.make_async_remote_copy(
            src_ref=t_send.at[1, pl.ds(0, N - 1)],
            dst_ref=t_back.at[pl.ds(0, N - 1)],
            send_sem=us_sem,
            recv_sem=ur_sem,
            device_id=to_tm(tm_peer(1)),
            device_id_type=MESH,
        )

    def each(peer, act):
        def body(j, carry):
            act(peer(j))
            return carry

        lax.fori_loop(1, N, body, 0)

    half_loaded(0).wait()
    pl.semaphore_wait(barrier, 2 * (N - 1))

    def send_spatial(c, d):
        parts = pack_spatial(c, d)
        for s in range(2):
            s_send[d, c, s] = parts[s]
        s_copy(c, d).start()

    half_loaded(1).wait()

    def pack_temporal(e):
        rows = pl.ds(pl.multiple_of((e // 4) * 16, 16), 16)
        cols = pl.ds(pl.multiple_of(512 + (e % 4) * 128, 128), 128)
        return [inp[a, :, rows, cols] for a in range(4)]

    def send_temporal(e):
        parts = pack_temporal(e)
        for a in range(4):
            t_send[0, e, a] = parts[a]
        t_copy(e).start()

    def both(j, carry):
        send_spatial(0, patch_peer(j))
        send_temporal(tm_peer(j))
        return carry

    lax.fori_loop(1, N, both, 0)
    each(patch_peer, lambda d: send_spatial(1, d))
    for c in range(2):
        parts = pack_spatial(c, me_p)
        for s in range(2):
            s_in[c, s, own_rows, :] = parts[s]
    parts = pack_temporal(me_t)
    for a in range(4):
        t_in[me_t, a] = parts[a]

    def spatial(c):
        s_all(c).wait_recv()
        low = lax.broadcasted_iota(jnp.int32, (QB, 128), 1) < 64

        def turn(i, carry):
            rows = pl.ds(pl.multiple_of(i * QB, QB), QB)
            a = s_in[c, 0, rows, :].astype(F32)
            tr_a[:, rows] = jnp.where(low, a * SCALE, a).T.astype(BF16)
            return carry

        lax.fori_loop(0, 1024 // QB, turn, 0)
        acc[...] = jnp.zeros_like(acc)

        def block(i, carry):
            rows = pl.ds(pl.multiple_of(i * QB, QB), QB)
            a = s_in[c, 0, rows, :]
            b = s_in[c, 1]
            zero = jnp.zeros_like(a)
            a_q = jnp.where(low, a * SCALE, zero)
            a_g = jnp.where(low, zero, a)
            scores = dot(a_q, b, 1, 1)
            weight_grad = dot(a_g, b, 1, 1)
            e = jnp.exp(scores - jnp.max(scores, axis=1, keepdims=True))
            inverse = 1.0 / jnp.sum(e, axis=1, keepdims=True)
            delta = jnp.sum(e * weight_grad, axis=1, keepdims=True) * inverse
            w = e * inverse
            ds_b = (w * (weight_grad - delta)).astype(BF16)
            w_b = w.astype(BF16)
            out = jnp.where(low, dot(ds_b, b, 1, 0) * SCALE, dot(w_b, b, 1, 0))
            s_out[c, 0, rows, :] = out.astype(BF16)
            acc[0:64, :] += dot(tr_a[0:64, rows], ds_b, 1, 0)
            acc[64:128, :] += dot(tr_a[64:128, rows], w_b, 1, 0)
            return carry

        lax.fori_loop(0, 1024 // QB, block, 0)

        def back(i, carry):
            rows = pl.ds(pl.multiple_of(i * QB, QB), QB)
            s_out[c, 1, rows, :] = acc[:, rows].T.astype(BF16)
            return carry

        lax.fori_loop(0, 1024 // QB, back, 0)
        def first(d, carry):
            @pl.when(d != me_p)
            def _():
                b_copy(c, d).start()

            return carry

        def later(j, carry):
            d = patch_peer(j)

            @pl.when(d >= 6)
            def _():
                b_copy(c, d).start()

            return carry

        lax.fori_loop(0, 6, first, 0)
        lax.fori_loop(1, N, later, 0)
        for s in range(2):
            s_back[me_p, c, s] = s_out[c, s, own_rows, :]

    def temporal():
        ws_copy.wait()
        t_all().wait_recv()

        def widen(e, carry):
            for a in range(4):
                rows = pl.ds(pl.multiple_of(e * 64, 64), 64)
                t_f32[a, rows, :] = t_in[e, a].reshape(64, 128).astype(F32)
            return carry

        lax.fori_loop(0, N, widen, 0)
        i0 = lax.broadcasted_iota(jnp.int32, (64, 64), 0)
        i1 = lax.broadcasted_iota(jnp.int32, (64, 64), 1)
        starts = jnp.sum(
            jnp.where(i0 == i1, jnp.broadcast_to(ws_ref[...].astype(F32), (64, 64)), 0.0),
            axis=1, keepdims=True,
        )
        lanes = lax.broadcasted_iota(jnp.int32, (64, 128), 1)
        low = lanes < 64
        frame = jnp.where(low, lanes, lanes - 64).astype(F32)
        allowed = (frame >= starts) & (frame < starts + WINDOW)
        allowed_0 = allowed & low
        allowed_1 = allowed & ~low

        def halves(x, op, fill, mask_0, mask_1):
            r0 = op(jnp.where(mask_0, x, fill), axis=1, keepdims=True)
            r1 = op(jnp.where(mask_1, x, fill), axis=1, keepdims=True)
            return jnp.where(low, r0, r1)

        def diagonal(x):
            return jnp.concatenate(
                [jnp.where(low, x, 0.0), jnp.where(low, 0.0, x)], axis=0
            ).astype(BF16)

        def patches(i, carry):
            group = [pl.ds(i * GROUP + u, 64, stride=16) for u in range(GROUP)]
            items = []
            for rows in group:
                q, k, v, g = (t_f32[a, rows, :] for a in range(4))
                items.append(((q * SCALE).astype(BF16), diagonal(k), diagonal(v), g.astype(BF16)))
            scores = [dot(q, k_d, 1, 1) for q, k_d, v_d, g in items]
            weight_grads = [dot(g, v_d, 1, 1) for q, k_d, v_d, g in items]
            highest = [halves(x, jnp.max, -1e30, allowed_0, allowed_1) for x in scores]
            exps = [
                jnp.where(allowed, jnp.exp(x - m), 0.0) for x, m in zip(scores, highest)
            ]
            ws = [e * (1.0 / halves(e, jnp.sum, 0.0, low, ~low)) for e in exps]
            deltas = [
                halves(w * x, jnp.sum, 0.0, low, ~low) for w, x in zip(ws, weight_grads)
            ]
            grads = [
                (w * (x - m)).astype(BF16) for w, x, m in zip(ws, weight_grads, deltas)
            ]
            ws = [w.astype(BF16) for w in ws]
            for rows, (q, k_d, v_d, g), w_b, ds_b in zip(group, items, ws, grads):
                dk = dot(ds_b, q, 0, 0)
                dv = dot(w_b, g, 0, 0)
                t_res[0, rows, :] = dot(w_b, v_d, 1, 0)
                t_res[1, rows, :] = dot(ds_b, k_d, 1, 0) * SCALE
                t_res[2, rows, :] = jnp.where(low, dk[:64], dk[64:])
                t_res[3, rows, :] = jnp.where(low, dv[:64], dv[64:])
            return carry

        lax.fori_loop(0, 16 // GROUP, patches, 0)

        def narrow(e):
            rows = pl.ds(pl.multiple_of(e * 64, 64), 64)
            return [t_res[a, rows, :].astype(BF16).reshape(4, 16, 128) for a in range(4)]

        def send_back(e):
            parts = narrow(e)
            for a in range(4):
                t_send[1, e, a] = parts[a]
            u_copy(e).start()

        each(tm_peer, send_back)
        parts = narrow(me_t)
        for a in range(4):
            t_back[me_t, a] = parts[a]

    spatial(0)
    temporal()
    spatial(1)

    outs = (o_ref, dq_ref, dk_ref, dv_ref)

    def unpack_temporal(e):
        rows = pl.ds(pl.multiple_of((e // 4) * 16, 16), 16)
        cols = pl.ds(pl.multiple_of(512 + (e % 4) * 128, 128), 128)
        for a in range(4):
            outs[a][0, :, rows, cols] = t_back[e, a]

    u_all().wait_recv()
    unpack_temporal(me_t)
    each(tm_peer, unpack_temporal)

    def unpack_spatial(d):
        f = d // 4
        cols = pl.ds(pl.multiple_of((d % 4) * 128, 128), 128)
        for s, (low_ref, high_ref) in enumerate(((dq_ref, o_ref), (dk_ref, dv_ref))):
            x, y = s_back[d, 0, s], s_back[d, 1, s]
            low_ref[0, f, :, cols] = jnp.concatenate([x[:, :64], y[:, :64]], axis=1)
            high_ref[0, f, :, cols] = jnp.concatenate([x[:, 64:], y[:, 64:]], axis=1)

    unpack_spatial(me_p)
    t_all().wait_send()
    u_all().wait_send()
    for c in range(2):
        s_all(c).wait_send()
    b_all(0).wait()

    def take_spatial(d):
        b_arrival(d).wait_recv()
        unpack_spatial(d)

    each(patch_peer, take_spatial)
    b_all(1).wait_send()


def emit(*refs):
    sem = refs[8]
    copies = [
        pltpu.make_async_copy(src, dst, sem.at[a])
        for a, (src, dst) in enumerate(zip(refs[:4], refs[4:8]))
    ]
    for copy in copies:
        copy.start()
    for copy in copies:
        copy.wait()


def on_device(queries, key_vectors, value_vectors, grad_output, window_start):
    anywhere = pl.BlockSpec(memory_space=pltpu.HBM)
    vmem = pl.BlockSpec(memory_space=pltpu.VMEM)
    dma = pltpu.SemaphoreType.DMA
    shape = jax.ShapeDtypeStruct((1, FR, PT, 1024), BF16)
    inputs = (queries, key_vectors, value_vectors, grad_output, window_start.reshape(1, 64))
    results = pl.pallas_call(
        kernel,
        out_shape=(shape,) * 4,
        in_specs=[anywhere] * 5,
        out_specs=(vmem,) * 4,
        scratch_shapes=[
            pltpu.VMEM((1, 64), jnp.int32),
            pltpu.VMEM((4, FR, PT, 1024), BF16),
            pltpu.VMEM((N, 2, 2, PT, 128), BF16),
            pltpu.VMEM((2, N, 4, FR, 16, 128), BF16),
            pltpu.VMEM((2, 2, 1024, 128), BF16),
            pltpu.VMEM((N, 4, FR, 16, 128), BF16),
            pltpu.VMEM((4, 1024, 128), F32),
            pltpu.VMEM((4, 1024, 128), F32),
            pltpu.VMEM((128, 1024), BF16),
            pltpu.VMEM((128, 1024), F32),
            pltpu.VMEM((2, 2, 1024, 128), BF16),
            pltpu.VMEM((N, 2, 2, PT, 128), BF16),
            pltpu.VMEM((N, 4, FR, 16, 128), BF16),
            dma, dma((2,)),
            dma((2,)), dma((2,)), dma, dma, dma((2,)), dma, dma((N,)), dma, dma,
        ],
        compiler_params=pltpu.CompilerParams(
            collective_id=0, has_side_effects=True, vmem_limit_bytes=48 << 20
        ),
        name="attention",
    )(*(pltpu.with_memory_space_constraint(x, pltpu.HBM) for x in inputs))
    return pl.pallas_call(
        emit,
        out_shape=(shape,) * 4,
        in_specs=[vmem] * 4,
        out_specs=(anywhere,) * 4,
        scratch_shapes=[dma((4,))],
        compiler_params=pltpu.CompilerParams(vmem_limit_bytes=6 << 20),
        name="emit",
    )(*(pltpu.with_memory_space_constraint(x, pltpu.VMEM) for x in results))


def solution(mesh):
    spec = P(None, "tm", "patch", None)
    return jax.shard_map(
        on_device,
        mesh=mesh,
        in_specs=(spec,) * 4 + (P(),),
        out_specs=(spec,) * 4,
        check_vma=False,
    )
```
